32 devices in a mesh: wide: 8 (over y, x, core), narrow: 4 (over z).
Axes of the slice: x: 2, y: 2, z: 4, core: 2. Of those that a mesh axis runs over, the one named last changes fastest.
Arguments:
- tokens: bfloat16 [4096, 2048], P(('wide', 'narrow')), may hold values from -6 to 6
- cotangent: bfloat16 [4096, 2048], P(('wide', 'narrow')), may hold values from -1.5 to 1.5
- gate_prob: float32 [4096], P(('wide', 'narrow')), may hold values from 0.2 to 1
- expert_ids: int32 [4096, 1], P(('wide', 'narrow')), may hold values from 0 to 31; in each aligned block of 128 rows (0 to 127, 128 to 255, ...) at most 6 rows name the same one
- keep_mask: int32 [4096], P(('wide', 'narrow')), may hold values 0 or 1
- w_gate: bfloat16 [32, 2048, 704], P(('wide', 'narrow')), may hold values from -0.125 to 0.125
- w_up: bfloat16 [32, 2048, 704], P(('wide', 'narrow')), may hold values from -0.125 to 0.125
- w_down: bfloat16 [32, 704, 2048], P(('wide', 'narrow')), may hold values from -0.21875 to 0.21875
Outputs:
- grad_tokens: bfloat16 [4096, 2048], P(('wide', 'narrow'))
- grad_prob: float32 [4096], P(('wide', 'narrow'))
- grad_gate: bfloat16 [32, 2048, 704], P(('wide', 'narrow'))
- grad_up: bfloat16 [32, 2048, 704], P(('wide', 'narrow'))
- grad_down: bfloat16 [32, 704, 2048], P(('wide', 'narrow'))
The draws below stay inside these ranges and needn't reach their ends.
Inputs may be any that keep to these rules, and one draw needn't show every extreme that they name: `expert_ids`: among the 128 rows of one device no expert is named more than 6 times; in every draw some device names some expert exactly 6 times.
All inputs are finite; a program needn't handle non-finite values. No bound on the sum of `keep_mask` on one device may be relied on, other than what follows from the above.
Results may differ from the reference program's by a relative error of at most 0.015.
Values may be sent and summed in bfloat16 or wider, within the bound.
A program may use at most 64 MiB of HBM per device.

```python
import math
import jax
import jax.numpy as jnp
import numpy as np
from jax import lax

D = 2048
H = 704
TOK_DEV = 128
EXPERTS = 32
TOKENS = 4096
CAP = 6
N_WIDE = 8
N_NARROW = 4


def plant(result, stream_key, least, largest):
    index_at = [jax.random.randint(jax.random.fold_in(stream_key, axis), (), 0, length) for axis, length in enumerate(result.shape)]
    widest = result.shape.index(max(result.shape))
    beside = index_at[:widest] + [(index_at[widest] + 1) % result.shape[widest]] + index_at[widest + 1:]
    return result.at[tuple(index_at)].set(least).at[tuple(beside)].set(largest)


def levels(own_key, extent, pieces, smallest, largest):
    def one(position, shards_of):
        heights = jax.random.uniform(jax.random.fold_in(jax.random.fold_in(own_key, 6), position), (shards_of,), jnp.float32, smallest / len(pieces), largest / len(pieces))
        return jnp.repeat(jnp.exp(heights), extent[position] // shards_of).reshape((-1,) + (1,) * (len(extent) - position - 1))

    level = one(*pieces[0])
    for cut in pieces[1:]:
        level = level * one(*cut)
    return level


def assign_block(stream_key, own, number, rows, number_of, top, bound, skew):
    order = jax.random.permutation(stream_key, number_of)
    packed, common = portions_of(number_of, rows * top, bound, skew, True), portions_of(number_of, rows * top, bound, skew, False)
    places = jnp.arange(number_of)

    def named(tallies, turn):
        used = int((tallies > 0).sum())
        fixed = max(1, used // 4)
        passed = fixed + (places - fixed + turn * (used - fixed)) % max(1, number_of - fixed)
        return jnp.zeros((number_of,), jnp.int32).at[order[jnp.where(places < fixed, places, passed)]].set(jnp.asarray(tallies, jnp.int32))

    tallies = jnp.where(number % 4 == 0, named(packed, number // 4), named(common, number - number // 4 - 1))
    mixed = jax.random.permutation(jax.random.fold_in(own, 3), number_of)
    source_of, receiver = mixed[0:number_of // 2 * 2:2], mixed[1:number_of // 2 * 2:2]
    margin = jnp.minimum(tallies[source_of] - 1, bound - tallies[receiver]) // 2
    margin = jnp.where((source_of == order[0]) | (receiver == order[0]) | (tallies[receiver] == 0), 0, jnp.maximum(margin, 0))
    passed = jax.random.randint(jax.random.fold_in(own, 4), (number_of // 2,), 0, 1 << 20) % (margin + 1)
    tallies = tallies.at[source_of].add(-passed).at[receiver].add(passed)
    members = jnp.searchsorted(jnp.cumsum(tallies), jnp.arange(rows * top), side="right").astype(jnp.int32)
    listing = members.reshape(top, rows).T
    listing = listing[jax.random.permutation(jax.random.fold_in(own, 1), rows)]
    turn = jax.random.randint(jax.random.fold_in(own, 2), (rows, 1), 0, top)
    return jnp.take_along_axis(listing, (jnp.arange(top)[None, :] + turn) % top, axis=1)


def portions_of(amount, total, reach, skew, full):
    portions = [(1 << 20) // math.isqrt(rank ** skew) + 1 for rank in range(1, amount + 1)]
    largest = reach if full else min(reach, max(-(-total // amount), total * portions[0] // sum(portions)))
    least = 1 if total - largest >= amount - 1 else 0
    holding, spare = [largest] + [least] * (amount - 1), total - largest - least * (amount - 1)
    while spare > 0:
        movable = [i for i in range(1, amount) if holding[i] < largest] or [i for i in range(1, amount) if holding[i] < reach]
        mass, budget = sum([portions[i] for i in movable]), spare
        for i in movable:
            extra = min(reach - holding[i], max(1, budget * portions[i] // mass), spare)
            holding[i] = holding[i] + extra
            spare = spare - extra
    return np.array(holding)


def normal_values(key, shape, width, most, split=(), kind=jnp.bfloat16):
    loudness = levels(key, shape, split, -0.22, 0.18) if split else 1.0
    result = jax.random.normal(key, shape, jnp.float32) * width * loudness
    return jnp.minimum(jnp.maximum(result, -most), most).astype(kind)


def setup_inputs(seed: int = 0) -> dict:
    arg_keys = jax.random.split(jax.random.key(seed), 9)
    tokens = normal_values(arg_keys[0], (TOKENS, D), 1.0, 6.0, ((0, 32),))
    cotangent = normal_values(arg_keys[1], (TOKENS, D), 0.25, 1.5, ((0, 32),))
    gate_prob = jnp.clip(0.2 + 0.8 * jax.random.uniform(arg_keys[2], (TOKENS,), jnp.float32) ** levels(arg_keys[2], (TOKENS,), ((0, 32),), -0.2, 0.2), 0.2, 1.0)
    expert_ids_keys = jax.random.split(jax.random.fold_in(arg_keys[3], 1), TOKENS // TOK_DEV)
    expert_ids_turns = jax.random.permutation(jax.random.fold_in(arg_keys[3], 3), TOKENS // TOK_DEV)
    expert_ids = jax.vmap(lambda own, number: assign_block(jax.random.fold_in(arg_keys[3], 2), own, number, TOK_DEV, EXPERTS, 1, CAP, 2))(expert_ids_keys, expert_ids_turns).reshape((TOKENS, 1))
    keep_mask = plant((jax.random.randint(arg_keys[4], (TOKENS,), 0, 8) < 7).astype(jnp.int32), jax.random.fold_in(arg_keys[4], 1), 0, 1)
    w_gate = normal_values(arg_keys[5], (EXPERTS, D, H), D ** -0.5, 0.125, ((0, 32),))
    w_up = normal_values(arg_keys[6], (EXPERTS, D, H), D ** -0.5, 0.125, ((0, 32),))
    w_down = normal_values(arg_keys[7], (EXPERTS, H, D), H ** -0.5, 0.21875, ((0, 32),))
    return {"tokens": tokens, "cotangent": cotangent, "gate_prob": gate_prob, "expert_ids": expert_ids, "keep_mask": keep_mask, "w_gate": w_gate, "w_up": w_up, "w_down": w_down}


def expert_grad(rows_in, rows_cot, rows_prob, wgate, wup, wdown):
    g = jnp.dot(rows_in, wgate, preferred_element_type=jnp.float32)
    u = jnp.dot(rows_in, wup, preferred_element_type=jnp.float32)
    sig = jax.nn.sigmoid(g)
    silu_g = g * sig
    hidden = (silu_g * u).astype(jnp.bfloat16)
    out_rows = jnp.dot(hidden, wdown, preferred_element_type=jnp.float32)
    prob_grad = lax.optimization_barrier(jnp.sum(rows_cot.astype(jnp.float32) * out_rows, axis=1))
    dout = (rows_prob[:, None] * rows_cot.astype(jnp.float32)).astype(jnp.bfloat16)
    gdown = lax.dot_general(hidden, dout, (((0,), (0,)), ((), ())), preferred_element_type=jnp.float32).astype(jnp.bfloat16)
    dhid = lax.dot_general(dout, wdown, (((1,), (1,)), ((), ())), preferred_element_type=jnp.float32)
    dgate = (dhid * u * sig * (1.0 + g * (1.0 - sig))).astype(jnp.bfloat16)
    dup = (dhid * silu_g).astype(jnp.bfloat16)
    ggate = lax.dot_general(rows_in, dgate, (((0,), (0,)), ((), ())), preferred_element_type=jnp.float32).astype(jnp.bfloat16)
    gup = lax.dot_general(rows_in, dup, (((0,), (0,)), ((), ())), preferred_element_type=jnp.float32).astype(jnp.bfloat16)
    dx_rows = lax.dot_general(dgate, wgate, (((1,), (1,)), ((), ())), preferred_element_type=jnp.float32)
    dx_rows = dx_rows + lax.dot_general(dup, wup, (((1,), (1,)), ((), ())), preferred_element_type=jnp.float32)
    return (dx_rows.astype(jnp.bfloat16), prob_grad, ggate, gup, gdown)

def reference(tokens, cotangent, gate_prob, expert_ids, keep_mask, w_gate, w_up, w_down):
    sources = N_WIDE * N_NARROW
    ids = expert_ids[:, 0].astype(jnp.int32)
    kept = keep_mask == 1
    onehot = ((ids[:, None] == jnp.arange(EXPERTS, dtype=jnp.int32)[None, :]) & kept[:, None]).astype(jnp.int32)
    onehot = onehot.reshape(sources, TOK_DEV, EXPERTS)
    before = jnp.cumsum(onehot, axis=1) - onehot
    slot = lax.optimization_barrier(jnp.sum(before * onehot, axis=2)).reshape(-1).astype(jnp.int32)
    source = (jnp.arange(TOKENS, dtype=jnp.int32) // TOK_DEV).astype(jnp.int32)
    row = (source * CAP + slot).astype(jnp.int32)
    dest = jnp.where(kept, ids, EXPERTS).astype(jnp.int32)
    total_rows = sources * CAP
    x_buf = jnp.zeros((EXPERTS, total_rows, D), jnp.bfloat16).at[dest, row].set(tokens, mode='drop')
    c_buf = jnp.zeros((EXPERTS, total_rows, D), jnp.bfloat16).at[dest, row].set(cotangent, mode='drop')
    p_buf = jnp.zeros((EXPERTS, total_rows), jnp.float32).at[dest, row].set(gate_prob, mode='drop')

    def one_expert(args):
        return expert_grad(*args)
    dx_buf, dp_buf, ggate, gup, gdown = lax.map(one_expert, (x_buf, c_buf, p_buf, w_gate, w_up, w_down))
    safe = jnp.minimum(dest, EXPERTS - 1).astype(jnp.int32)
    grad_tokens = jnp.where(kept[:, None], dx_buf[safe, row], jnp.zeros((), jnp.bfloat16)).astype(jnp.bfloat16)
    grad_prob = jnp.where(kept, dp_buf[safe, row], jnp.zeros((), jnp.float32))
    return (grad_tokens, grad_prob, ggate, gup, gdown)
```

```python
import functools

import jax
import jax.numpy as jnp
import numpy as np
from jax import lax
from jax.experimental import pallas as pl
from jax.experimental.pallas import tpu as pltpu
from jax.sharding import PartitionSpec as P

GROUP = 8
PIECES = 8
MESH = pl.DeviceIdType.MESH
NT = (((1,), (1,)), ((), ()))
TN = (((0,), (0,)), ((), ()))


def f32dot(a, b, dims=(((1,), (0,)), ((), ()))):
    return lax.dot_general(a, b, dims, preferred_element_type=jnp.float32)


def exchange_kernel(
    n, n_narrow, cap,
    tok_ref, cot_ref, prob_ref, tgt_row_ref, tgt_ref, eid_ref, slot_ref, perm_ref,
    wg_hbm, wu_hbm, wd_hbm,
    gtok_ref, gprob_ref, x_ref, d_ref, h_ref, dg_ref, du_ref,
    wg, wu, wd, xstack, dstack, cstack,
    xsend, dsend, bsend, xrecv, drecv, brecv, psend, precv, pmat,
    wsem, xs, xr, ds, dr, bs, br, ps, pr,
):
    wide, narrow = lax.axis_index("wide"), lax.axis_index("narrow")
    me = wide * n_narrow + narrow
    groups = n // GROUP
    mine = me // GROUP
    lane = me % GROUP
    tok = tok_ref.shape[0]
    piece = tok_ref.shape[1] // PIECES
    rows = GROUP * cap
    block = cap * PIECES

    loads = [
        pltpu.make_async_copy(src, dst, wsem.at[i])
        for i, (src, dst) in enumerate(((wg_hbm, wg), (wu_hbm, wu), (wd_hbm, wd)))
    ]
    for load in loads:
        load.start()

    def where(d):
        return (d // n_narrow, d % n_narrow)

    barrier = pltpu.get_barrier_semaphore()

    @pl.loop(1, n)
    def _(i):
        pl.semaphore_signal(
            barrier, inc=1, device_id=where((me + i) % n), device_id_type=MESH
        )

    for k in range(PIECES):
        cols = slice(k * piece, (k + 1) * piece)
        at = slice(k * tok, (k + 1) * tok)
        xstack[at, :] = tok_ref[:, cols]
        dstack[at, :] = (prob_ref[...] * cot_ref[:, cols].astype(jnp.float32)).astype(
            jnp.bfloat16
        )

    def copy(send, recv, ss, rs, d):
        return pltpu.make_async_remote_copy(
            src_ref=send.at[d], dst_ref=recv.at[me], send_sem=ss.at[d],
            recv_sem=rs.at[me], device_id=where(d), device_id_type=MESH,
        )

    def arrival(send, recv, ss, rs, s):
        return pltpu.make_async_remote_copy(
            src_ref=send.at[s], dst_ref=recv.at[s], send_sem=ss.at[s],
            recv_sem=rs.at[s], device_id=where(s), device_id_type=MESH,
        )

    def fill(i, first):
        g = (mine - i + groups) % groups
        base = g * GROUP
        at = lax.broadcasted_iota(jnp.int32, (GROUP * block, tok), 0) + base * block
        route = jnp.concatenate(
            [
                (at == tgt_row_ref[...] + k).astype(jnp.float32).astype(jnp.bfloat16)
                for k in range(PIECES)
            ],
            axis=1,
        )
        xsend[pl.ds(base, GROUP)] = (
            f32dot(route, xstack[...]).astype(jnp.bfloat16).reshape(GROUP, block, piece)
        )
        dsend[pl.ds(base, GROUP)] = (
            f32dot(route, dstack[...]).astype(jnp.bfloat16).reshape(GROUP, block, piece)
        )
        if first:
            pl.semaphore_wait(barrier, n - 1)

        for send, recv, ss, rs in ((xsend, xrecv, xs, xr), (dsend, drecv, ds, dr)):

            @pl.loop(0, GROUP)
            def _(q):
                d = base + (lane + q) % GROUP

                @pl.when(d != me)
                def _():
                    copy(send, recv, ss, rs, d).start()

    fill(0, True)
    xrecv[me] = xsend[me]
    drecv[me] = dsend[me]

    @pl.loop(1, groups)
    def _(i):
        fill(i, False)

    for load in loads:
        load.wait()

    spread = lax.broadcasted_iota(jnp.int32, (rows, 128), 0) % cap
    keep = spread == lax.broadcasted_iota(jnp.int32, (rows, 128), 1)
    owner = lax.broadcasted_iota(jnp.int32, (GROUP, rows), 1) // cap
    gather = (owner == lax.broadcasted_iota(jnp.int32, (GROUP, rows), 0)).astype(jnp.float32)

    def take(send, recv, ss, rs, base, out_ref, at):
        @pl.loop(0, GROUP)
        def _(q):
            s = base + q

            @pl.when(s != me)
            def _():
                arrival(send, recv, ss, rs, s).wait_recv()

        got = recv[pl.ds(base, GROUP)].reshape(GROUP * block, piece)
        got = f32dot(perm_ref[...], got).astype(jnp.bfloat16)
        for k in range(PIECES):
            out_ref[at, k * piece:(k + 1) * piece] = got[k * rows:(k + 1) * rows]

    @pl.loop(0, groups)
    def _(i):
        base = ((mine + i) % groups) * GROUP
        at = pl.ds(pl.multiple_of(i * rows, rows), rows)
        take(xsend, xrecv, xs, xr, base, x_ref, at)
        x = x_ref[at, :]
        g = f32dot(x, wg[...])
        u = f32dot(x, wu[...])
        sig = 1.0 / (1.0 + jnp.exp(-g))
        silu = g * sig
        h = (silu * u).astype(jnp.bfloat16)
        h_ref[at, :] = h
        take(dsend, drecv, ds, dr, base, d_ref, at)
        dh = f32dot(d_ref[at, :], wd[...], NT)
        total = jnp.sum(h.astype(jnp.float32) * dh, axis=1, keepdims=True)
        dg = (dh * u * sig * (1.0 + g * (1.0 - sig))).astype(jnp.bfloat16)
        du = (dh * silu).astype(jnp.bfloat16)
        dg_ref[at, :] = dg
        du_ref[at, :] = du
        dx = (f32dot(dg, wg[...], NT) + f32dot(du, wu[...], NT)).astype(jnp.bfloat16)
        for k in range(PIECES):
            cstack[k * rows:(k + 1) * rows, :] = dx[:, k * piece:(k + 1) * piece]
        bsend[pl.ds(base, GROUP)] = (
            f32dot(perm_ref[...], cstack[...], TN)
            .astype(jnp.bfloat16)
            .reshape(GROUP, block, piece)
        )
        probs = lax.dot_general(
            gather, jnp.where(keep, total, 0.0), (((1,), (0,)), ((), ())),
            precision=lax.Precision.HIGHEST, preferred_element_type=jnp.float32,
        )
        for q in range(GROUP):
            psend[base + q] = probs[q:q + 1]

        @pl.loop(0, GROUP)
        def _(q):
            d = base + (lane + q) % GROUP

            @pl.when(d != me)
            def _():
                copy(bsend, brecv, bs, br, d).start()
                copy(psend, precv, ps, pr, d).start()

        @pl.when(i == 0)
        def _():
            brecv[me] = bsend[me]
            precv[me] = psend[me]

    @pl.loop(0, n)
    def _(s):
        @pl.when(s != me)
        def _():
            arrival(bsend, brecv, bs, br, s).wait_recv()
            arrival(psend, precv, ps, pr, s).wait_recv()

        pmat[pl.ds(s, 1), :] = precv[s]

    back = brecv[...].reshape(n * block, piece)
    at = lax.broadcasted_iota(jnp.int32, (tok, n * block), 1)
    for k in range(PIECES):
        route = (at == tgt_ref[...] + k).astype(jnp.float32).astype(jnp.bfloat16)
        gtok_ref[:, k * piece:(k + 1) * piece] = f32dot(route, back).astype(jnp.bfloat16)
    pick = (lax.broadcasted_iota(jnp.int32, (tok, n), 1) == eid_ref[...]).astype(jnp.float32)
    found = lax.dot_general(
        pick, pmat[...], (((1,), (0,)), ((), ())),
        precision=lax.Precision.HIGHEST, preferred_element_type=jnp.float32,
    )
    found = jnp.where(
        lax.broadcasted_iota(jnp.int32, (tok, 128), 1) == slot_ref[...], found, 0.0
    )
    gprob_ref[...] = jnp.sum(found, axis=1, keepdims=True) / prob_ref[...]

    @pl.loop(0, n)
    def _(d):
        @pl.when(d != me)
        def _():
            copy(xsend, xrecv, xs, xr, d).wait_send()
            copy(dsend, drecv, ds, dr, d).wait_send()
            copy(bsend, brecv, bs, br, d).wait_send()
            copy(psend, precv, ps, pr, d).wait_send()


def weight_kernel(x_ref, d_ref, h_ref, dg_ref, du_ref, gg_ref, gu_ref, gd_ref):
    x = x_ref[...]
    gg_ref[0] = f32dot(x, dg_ref[...], TN).astype(jnp.bfloat16)
    gu_ref[0] = f32dot(x, du_ref[...], TN).astype(jnp.bfloat16)
    gd_ref[0] = f32dot(h_ref[...], d_ref[...], TN).astype(jnp.bfloat16)


def on_device(tokens, cotangent, gate_prob, expert_ids, keep_mask, w_gate, w_up, w_down):
    tok, width = tokens.shape
    hidden = w_gate.shape[2]
    n_wide, n_narrow = lax.axis_size("wide"), lax.axis_size("narrow")
    n = n_wide * n_narrow
    cap = max(2, 5 * tok // (4 * n) + 1)
    piece = width // PIECES
    block = cap * PIECES
    rows = GROUP * cap

    ids = expert_ids[:, 0]
    kept = keep_mask == 1
    order = jnp.arange(tok, dtype=jnp.int32)
    earlier = (ids[:, None] == ids[None, :]) & kept[None, :] & (order[None, :] < order[:, None])
    slot = jnp.sum(earlier.astype(jnp.int32), axis=1)
    target = jnp.where(kept, ids * block + slot * PIECES, -block)
    owner = jnp.where(kept, ids, -1)

    r = np.arange(GROUP * block)
    source, rest = r // block, r % block
    perm = np.zeros((GROUP * block, GROUP * block), np.float32)
    perm[(rest % PIECES) * rows + source * cap + rest // PIECES, r] = 1.0

    vmem = pl.BlockSpec(memory_space=pltpu.VMEM)
    hbm = pl.BlockSpec(memory_space=pl.ANY)
    bf16, f32 = jnp.bfloat16, jnp.float32
    buf = pltpu.VMEM((n, block, piece), bf16)
    small = pltpu.VMEM((n, 1, 128), f32)
    gtok, gprob, x, d, h, dg, du = pl.pallas_call(
        functools.partial(exchange_kernel, n, n_narrow, cap),
        out_shape=(
            jax.ShapeDtypeStruct((tok, width), bf16),
            jax.ShapeDtypeStruct((tok, 1), f32),
            jax.ShapeDtypeStruct((n * cap, width), bf16),
            jax.ShapeDtypeStruct((n * cap, width), bf16),
            jax.ShapeDtypeStruct((n * cap, hidden), bf16),
            jax.ShapeDtypeStruct((n * cap, hidden), bf16),
            jax.ShapeDtypeStruct((n * cap, hidden), bf16),
        ),
        in_specs=[vmem] * 8 + [hbm] * 3,
        out_specs=(vmem,) * 7,
        scratch_shapes=[
            pltpu.VMEM((width, hidden), bf16),
            pltpu.VMEM((width, hidden), bf16),
            pltpu.VMEM((hidden, width), bf16),
            pltpu.VMEM((PIECES * tok, piece), bf16),
            pltpu.VMEM((PIECES * tok, piece), bf16),
            pltpu.VMEM((GROUP * block, piece), bf16),
            buf, buf, buf, buf, buf, buf, small, small,
            pltpu.VMEM((n, 128), f32),
            pltpu.SemaphoreType.DMA((3,)),
        ] + [pltpu.SemaphoreType.DMA((n,))] * 8,
        compiler_params=pltpu.CompilerParams(
            collective_id=0, has_side_effects=True, vmem_limit_bytes=48 * 1024 * 1024
        ),
        name="exchange",
    )(
        tokens, cotangent, gate_prob[:, None], target[None, :], target[:, None],
        owner[:, None], slot[:, None], jnp.asarray(perm, bf16),
        w_gate[0], w_up[0], w_down[0],
    )

    tile = 256
    full = pl.BlockSpec((n * cap, hidden), lambda i: (0, 0))
    part = pl.BlockSpec((n * cap, tile), lambda i: (0, i))
    ggate, gup, gdown = pl.pallas_call(
        weight_kernel,
        grid=(width // tile,),
        out_shape=(
            jax.ShapeDtypeStruct((1, width, hidden), bf16),
            jax.ShapeDtypeStruct((1, width, hidden), bf16),
            jax.ShapeDtypeStruct((1, hidden, width), bf16),
        ),
        in_specs=[part, part, full, full, full],
        out_specs=(
            pl.BlockSpec((1, tile, hidden), lambda i: (0, i, 0)),
            pl.BlockSpec((1, tile, hidden), lambda i: (0, i, 0)),
            pl.BlockSpec((1, hidden, tile), lambda i: (0, 0, i)),
        ),
        compiler_params=pltpu.CompilerParams(vmem_limit_bytes=32 * 1024 * 1024),
        name="weights",
    )(x, d, h, dg, du)
    return gtok, gprob[:, 0], ggate, gup, gdown


def solution(mesh):
    both = ("wide", "narrow")
    return jax.shard_map(
        on_device,
        mesh=mesh,
        in_specs=(
            P(both, None), P(both, None), P(both), P(both, None), P(both),
            P(both, None, None), P(both, None, None), P(both, None, None),
        ),
        out_specs=(
            P(both, None), P(both),
            P(both, None, None), P(both, None, None), P(both, None, None),
        ),
        check_vma=False,
    )
```

```python
import functools

import jax
import jax.numpy as jnp
import numpy as np
from jax import lax
from jax.experimental import pallas as pl
from jax.experimental.pallas import tpu as pltpu
from jax.sharding import PartitionSpec as P

GROUP = 8
PIECES = 8
MESH = pl.DeviceIdType.MESH
NT = (((1,), (1,)), ((), ()))
TN = (((0,), (0,)), ((), ()))


def f32dot(a, b, dims=(((1,), (0,)), ((), ()))):
    return lax.dot_general(a, b, dims, preferred_element_type=jnp.float32)


def exchange_kernel(
    n, n_narrow, cap,
    tok_ref, cot_ref, prob_ref, ids_ref, keep_ref, perm_ref, unperm_ref,
    wg_hbm, wu_hbm, wd_hbm,
    gtok_ref, gprob_ref, gg_ref, gu_ref, gd_ref,
    wg, wu, wd, xstack, dstack, cstack, x_ref, d_ref, h_ref, dg_ref, du_ref, turned,
    xsend, dsend, bsend, xrecv, drecv, brecv, psend, precv, pmat,
    wsem, xs, xr, ds, dr, bs, br, ps, pr,
):
    wide, narrow = lax.axis_index("wide"), lax.axis_index("narrow")
    me = wide * n_narrow + narrow
    groups = n // GROUP
    mine = me // GROUP
    lane = me % GROUP
    tok = tok_ref.shape[0]
    piece = tok_ref.shape[1] // PIECES
    rows = GROUP * cap
    block = cap * PIECES

    loads = [
        pltpu.make_async_copy(src, dst, wsem.at[i])
        for i, (src, dst) in enumerate(((wg_hbm, wg), (wu_hbm, wu), (wd_hbm, wd)))
    ]
    for load in loads:
        load.start()

    def where(d):
        return (d // n_narrow, d % n_narrow)

    barrier = pltpu.get_barrier_semaphore()

    @pl.loop(1, n)
    def _(i):
        pl.semaphore_signal(
            barrier, inc=1, device_id=where((me + i) % n), device_id_type=MESH
        )

    older = lax.broadcasted_iota(jnp.int32, (tok, tok), 0)
    newer = lax.broadcasted_iota(jnp.int32, (tok, tok), 1)
    eye = older == newer

    def column(row):
        return jnp.sum(jnp.where(eye, row, 0.0), axis=1, keepdims=True)

    eid_row = jnp.where(keep_ref[...] == 1, ids_ref[...], -1).astype(jnp.float32)
    eid = column(eid_row)
    same = eid == eid_row
    slot_row = jnp.sum(
        jnp.where(same & (older < newer), 1.0, 0.0), axis=0, keepdims=True
    )
    slot = jnp.sum(jnp.where(same & (newer < older), 1.0, 0.0), axis=1, keepdims=True)

    def target(e, j):
        return jnp.where(e >= 0.0, e * block + j * PIECES, -1.0 * block).astype(jnp.int32)

    tgt_row, tgt = target(eid_row, slot_row), target(eid, slot)
    prob = column(prob_ref[...])

    for k in range(PIECES):
        cols = slice(k * piece, (k + 1) * piece)
        at = slice(k * tok, (k + 1) * tok)
        xstack[at, :] = tok_ref[:, cols]
        dstack[at, :] = (prob * cot_ref[:, cols].astype(jnp.float32)).astype(
            jnp.bfloat16
        )

    def copy(send, recv, ss, rs, d):
        return pltpu.make_async_remote_copy(
            src_ref=send.at[d], dst_ref=recv.at[me], send_sem=ss.at[d],
            recv_sem=rs.at[me], device_id=where(d), device_id_type=MESH,
        )

    def arrival(send, recv, ss, rs, s):
        return pltpu.make_async_remote_copy(
            src_ref=send.at[s], dst_ref=recv.at[s], send_sem=ss.at[s],
            recv_sem=rs.at[s], device_id=where(s), device_id_type=MESH,
        )

    def fill(i, first):
        g = (mine - i + groups) % groups
        base = g * GROUP
        at = lax.broadcasted_iota(jnp.int32, (GROUP * block, tok), 0) + base * block
        route = jnp.concatenate(
            [
                (at == tgt_row + k).astype(jnp.float32).astype(jnp.bfloat16)
                for k in range(PIECES)
            ],
            axis=1,
        )
        xsend[pl.ds(base, GROUP)] = (
            f32dot(route, xstack[...]).astype(jnp.bfloat16).reshape(GROUP, block, piece)
        )
        dsend[pl.ds(base, GROUP)] = (
            f32dot(route, dstack[...]).astype(jnp.bfloat16).reshape(GROUP, block, piece)
        )
        if first:
            pl.semaphore_wait(barrier, n - 1)

        for send, recv, ss, rs in ((xsend, xrecv, xs, xr), (dsend, drecv, ds, dr)):

            @pl.loop(0, GROUP)
            def _(q):
                d = base + (lane + q) % GROUP

                @pl.when(d != me)
                def _():
                    copy(send, recv, ss, rs, d).start()

    fill(0, True)
    xrecv[me] = xsend[me]
    drecv[me] = dsend[me]

    @pl.loop(1, groups)
    def _(i):
        fill(i, False)

    for load in loads:
        load.wait()

    spread = lax.broadcasted_iota(jnp.int32, (rows, 128), 0) % cap
    keep = spread == lax.broadcasted_iota(jnp.int32, (rows, 128), 1)
    owner = lax.broadcasted_iota(jnp.int32, (GROUP, rows), 1) // cap
    gather = (owner == lax.broadcasted_iota(jnp.int32, (GROUP, rows), 0)).astype(jnp.float32)

    def take(send, recv, ss, rs, base, out_ref, at):
        @pl.loop(0, GROUP)
        def _(q):
            s = base + q

            @pl.when(s != me)
            def _():
                arrival(send, recv, ss, rs, s).wait_recv()

        got = recv[pl.ds(base, GROUP)].reshape(GROUP * block, piece)
        got = f32dot(perm_ref[...], got).astype(jnp.bfloat16)
        for k in range(PIECES):
            out_ref[at, k * piece:(k + 1) * piece] = got[k * rows:(k + 1) * rows]

    @pl.loop(0, groups)
    def _(i):
        base = ((mine + i) % groups) * GROUP
        at = pl.ds(pl.multiple_of(i * rows, rows), rows)
        take(xsend, xrecv, xs, xr, base, x_ref, at)
        x = x_ref[at, :]
        g = f32dot(x, wg[...], NT)
        u = f32dot(x, wu[...], NT)
        sig = 1.0 / (1.0 + jnp.exp(-g))
        silu = g * sig
        h = (silu * u).astype(jnp.bfloat16)
        h_ref[at, :] = h
        take(dsend, drecv, ds, dr, base, d_ref, at)
        dh = f32dot(d_ref[at, :], wd[...], NT)
        total = jnp.sum(h.astype(jnp.float32) * dh, axis=1, keepdims=True)
        dg = (dh * u * sig * (1.0 + g * (1.0 - sig))).astype(jnp.bfloat16)
        du = (dh * silu).astype(jnp.bfloat16)
        dg_ref[at, :] = dg
        du_ref[at, :] = du
        dx = (f32dot(dg, wg[...]) + f32dot(du, wu[...])).astype(jnp.bfloat16)
        for k in range(PIECES):
            cstack[k * rows:(k + 1) * rows, :] = dx[:, k * piece:(k + 1) * piece]
        bsend[pl.ds(base, GROUP)] = (
            f32dot(unperm_ref[...], cstack[...])
            .astype(jnp.bfloat16)
            .reshape(GROUP, block, piece)
        )
        probs = lax.dot_general(
            gather, jnp.where(keep, total, 0.0), (((1,), (0,)), ((), ())),
            precision=lax.Precision.HIGHEST, preferred_element_type=jnp.float32,
        )
        for q in range(GROUP):
            psend[base + q] = probs[q:q + 1]

        @pl.loop(0, GROUP)
        def _(q):
            d = base + (lane + q) % GROUP

            @pl.when(d != me)
            def _():
                copy(bsend, brecv, bs, br, d).start()
                copy(psend, precv, ps, pr, d).start()

        @pl.when(i == 0)
        def _():
            brecv[me] = bsend[me]
            precv[me] = psend[me]

    for left, right_ref, out_ref in (
        (dg_ref, x_ref, gg_ref), (du_ref, x_ref, gu_ref), (h_ref, d_ref, gd_ref)
    ):
        turned[...] = left[...].T

        @pl.loop(0, PIECES)
        def _(k):
            cols = pl.ds(pl.multiple_of(k * piece, piece), piece)
            out_ref[:, cols] = f32dot(turned[...], right_ref[:, cols]).astype(jnp.bfloat16)

    @pl.loop(0, n)
    def _(s):
        @pl.when(s != me)
        def _():
            arrival(bsend, brecv, bs, br, s).wait_recv()
            arrival(psend, precv, ps, pr, s).wait_recv()

        pmat[pl.ds(s, 1), :] = precv[s]

    back = brecv[...].reshape(n * block, piece)
    at = lax.broadcasted_iota(jnp.int32, (tok, n * block), 1)
    for k in range(PIECES):
        route = (at == tgt + k).astype(jnp.float32).astype(jnp.bfloat16)
        gtok_ref[:, k * piece:(k + 1) * piece] = f32dot(route, back).astype(jnp.bfloat16)
    pick = (lax.broadcasted_iota(jnp.int32, (tok, n), 1) == eid.astype(jnp.int32)).astype(jnp.float32)
    found = lax.dot_general(
        pick, pmat[...], (((1,), (0,)), ((), ())),
        precision=lax.Precision.HIGHEST, preferred_element_type=jnp.float32,
    )
    found = jnp.where(
        lax.broadcasted_iota(jnp.int32, (tok, 128), 1) == slot.astype(jnp.int32), found, 0.0
    )
    found = jnp.sum(found, axis=1, keepdims=True)
    gprob_ref[...] = jnp.sum(jnp.where(eye, found, 0.0), axis=0, keepdims=True) / prob_ref[...]

    @pl.loop(0, n)
    def _(d):
        @pl.when(d != me)
        def _():
            copy(xsend, xrecv, xs, xr, d).wait_send()
            copy(dsend, drecv, ds, dr, d).wait_send()
            copy(bsend, brecv, bs, br, d).wait_send()
            copy(psend, precv, ps, pr, d).wait_send()


def on_device(tokens, cotangent, gate_prob, expert_ids, keep_mask, w_gate, w_up, w_down):
    tok, width = tokens.shape
    hidden = w_gate.shape[2]
    n_wide, n_narrow = lax.axis_size("wide"), lax.axis_size("narrow")
    n = n_wide * n_narrow
    cap = max(2, 5 * tok // (4 * n) + 1)
    piece = width // PIECES
    block = cap * PIECES
    rows = GROUP * cap

    r = np.arange(GROUP * block)
    source, rest = r // block, r % block
    perm = np.zeros((GROUP * block, GROUP * block), np.float32)
    perm[(rest % PIECES) * rows + source * cap + rest // PIECES, r] = 1.0

    vmem = pl.BlockSpec(memory_space=pltpu.VMEM)
    hbm = pl.BlockSpec(memory_space=pl.ANY)
    bf16, f32 = jnp.bfloat16, jnp.float32
    buf = pltpu.VMEM((n, block, piece), bf16)
    small = pltpu.VMEM((n, 1, 128), f32)
    weight = pltpu.VMEM((hidden, width), bf16)
    inner = pltpu.VMEM((n * cap, hidden), bf16)
    gtok, gprob, ggate, gup, gdown = pl.pallas_call(
        functools.partial(exchange_kernel, n, n_narrow, cap),
        out_shape=(
            jax.ShapeDtypeStruct((tok, width), bf16),
            jax.ShapeDtypeStruct((1, tok), f32),
            jax.ShapeDtypeStruct((hidden, width), bf16),
            jax.ShapeDtypeStruct((hidden, width), bf16),
            jax.ShapeDtypeStruct((hidden, width), bf16),
        ),
        in_specs=[vmem] * 7 + [hbm] * 3,
        out_specs=(vmem,) * 5,
        scratch_shapes=[
            weight, weight, weight,
            pltpu.VMEM((PIECES * tok, piece), bf16),
            pltpu.VMEM((PIECES * tok, piece), bf16),
            pltpu.VMEM((GROUP * block, piece), bf16),
            pltpu.VMEM((n * cap, width), bf16),
            pltpu.VMEM((n * cap, width), bf16),
            inner, inner, inner,
            pltpu.VMEM((hidden, n * cap), bf16),
            buf, buf, buf, buf, buf, buf, small, small,
            pltpu.VMEM((n, 128), f32),
            pltpu.SemaphoreType.DMA((3,)),
        ] + [pltpu.SemaphoreType.DMA((n,))] * 8,
        compiler_params=pltpu.CompilerParams(
            collective_id=0, has_side_effects=True, vmem_limit_bytes=42 * 1024 * 1024
        ),
        name="exchange",
    )(
        tokens, cotangent, gate_prob[None, :], expert_ids.reshape(1, tok), keep_mask[None, :],
        jnp.asarray(perm, bf16), jnp.asarray(perm.T, bf16),
        w_gate[0].T, w_up[0].T, w_down[0],
    )
    return gtok, gprob[0], ggate.T[None], gup.T[None], gdown[None]


def solution(mesh):
    both = ("wide", "narrow")
    return jax.shard_map(
        on_device,
        mesh=mesh,
        in_specs=(
            P(both, None), P(both, None), P(both), P(both, None), P(both),
            P(both, None, None), P(both, None, None), P(both, None, None),
        ),
        out_specs=(
            P(both, None), P(both),
            P(both, None, None), P(both, None, None), P(both, None, None),
        ),
        check_vma=False,
    )
```

```python
import functools

import jax
import jax.numpy as jnp
from jax import lax
from jax.experimental import pallas as pl
from jax.experimental.pallas import tpu as pltpu
from jax.sharding import PartitionSpec as P

GROUP = 8
PIECES = 8
MESH = pl.DeviceIdType.MESH
NT = (((1,), (1,)), ((), ()))
TN = (((0,), (0,)), ((), ()))


def f32dot(a, b, dims=(((1,), (0,)), ((), ()))):
    return lax.dot_general(a, b, dims, preferred_element_type=jnp.float32)


def exchange_kernel(
    n, n_narrow, cap,
    tok_ref, cot_ref, row_ref,
    wg_hbm, wu_hbm, wd_hbm,
    gtok_ref, gprob_ref, gg_ref, gu_ref, gd_ref,
    wg, wu, wd, xstack, dstack, cstack, x_ref, d_ref, h_ref, dg_ref, du_ref, turned,
    perm_ref, unperm_ref, gsum,
    xsend, dsend, bsend, xrecv, drecv, brecv, psend, precv, pmat,
    wsem, xs, xr, ds, dr, bs, br, ps, pr,
):
    wide, narrow = lax.axis_index("wide"), lax.axis_index("narrow")
    me = wide * n_narrow + narrow
    groups = n // GROUP
    mine = me // GROUP
    lane = me % GROUP
    tok = tok_ref.shape[0]
    piece = tok_ref.shape[1] // PIECES
    rows = GROUP * cap
    block = cap * PIECES

    loads = [
        pltpu.make_async_copy(src, dst, wsem.at[i])
        for i, (src, dst) in enumerate(((wg_hbm, wg), (wu_hbm, wu), (wd_hbm, wd)))
    ]
    for load in loads:
        load.start()

    def where(d):
        return (d // n_narrow, d % n_narrow)

    barrier = pltpu.get_barrier_semaphore()

    @pl.loop(1, n)
    def _(i):
        pl.semaphore_signal(
            barrier, inc=1, device_id=where((me + i) % n), device_id_type=MESH
        )

    older = lax.broadcasted_iota(jnp.int32, (tok, tok), 0)
    newer = lax.broadcasted_iota(jnp.int32, (tok, tok), 1)
    eye = older == newer

    def column(row):
        return jnp.sum(jnp.where(eye, row, 0.0), axis=1, keepdims=True)

    prob_row, eid_row = row_ref[0:1, :], row_ref[1:2, :]
    eid = column(eid_row)
    same = eid == eid_row
    slot_row = jnp.sum(
        jnp.where(same & (older < newer), 1.0, 0.0), axis=0, keepdims=True
    )
    slot = jnp.sum(jnp.where(same & (newer < older), 1.0, 0.0), axis=1, keepdims=True)

    def target(e, j):
        return jnp.where(e >= 0.0, e * block + j * PIECES, -1.0 * block).astype(jnp.int32)

    tgt_row, tgt = target(eid_row, slot_row), target(eid, slot)
    prob = column(prob_row)

    for k in range(PIECES):
        cols = slice(k * piece, (k + 1) * piece)
        at = slice(k * tok, (k + 1) * tok)
        xstack[at, :] = tok_ref[:, cols]
        dstack[at, :] = (prob * cot_ref[:, cols].astype(jnp.float32)).astype(
            jnp.bfloat16
        )

    def copy(send, recv, ss, rs, d):
        return pltpu.make_async_remote_copy(
            src_ref=send.at[d], dst_ref=recv.at[me], send_sem=ss.at[d],
            recv_sem=rs.at[me], device_id=where(d), device_id_type=MESH,
        )

    def arrival(send, recv, ss, rs, s):
        return pltpu.make_async_remote_copy(
            src_ref=send.at[s], dst_ref=recv.at[s], send_sem=ss.at[s],
            recv_sem=rs.at[s], device_id=where(s), device_id_type=MESH,
        )

    def fill(i, first):
        g = (mine - i + groups) % groups
        base = g * GROUP
        at = lax.broadcasted_iota(jnp.int32, (GROUP * block, tok), 0) + base * block
        route = jnp.concatenate(
            [
                (at == tgt_row + k).astype(jnp.float32).astype(jnp.bfloat16)
                for k in range(PIECES)
            ],
            axis=1,
        )
        xsend[pl.ds(base, GROUP)] = (
            f32dot(route, xstack[...]).astype(jnp.bfloat16).reshape(GROUP, block, piece)
        )
        dsend[pl.ds(base, GROUP)] = (
            f32dot(route, dstack[...]).astype(jnp.bfloat16).reshape(GROUP, block, piece)
        )
        if first:
            pl.semaphore_wait(barrier, n - 1)

        for send, recv, ss, rs in ((xsend, xrecv, xs, xr), (dsend, drecv, ds, dr)):

            @pl.loop(0, GROUP)
            def _(q):
                d = base + (lane + q) % GROUP

                @pl.when(d != me)
                def _():
                    copy(send, recv, ss, rs, d).start()

    fill(0, True)
    xrecv[me] = xsend[me]
    drecv[me] = dsend[me]

    @pl.loop(1, groups)
    def _(i):
        fill(i, False)

    size = GROUP * block
    one = lax.broadcasted_iota(jnp.int32, (size, size), 0)
    other = lax.broadcasted_iota(jnp.int32, (size, size), 1)
    for a, b, out in ((one, other, perm_ref), (other, one, unperm_ref)):
        hit = b == (a % rows) * PIECES + a // rows
        out[...] = hit.astype(jnp.float32).astype(jnp.bfloat16)

    for load in loads:
        load.wait()

    spread = lax.broadcasted_iota(jnp.int32, (rows, 128), 0) % cap
    keep = spread == lax.broadcasted_iota(jnp.int32, (rows, 128), 1)
    owner = lax.broadcasted_iota(jnp.int32, (GROUP, rows), 1) // cap
    gather = (owner == lax.broadcasted_iota(jnp.int32, (GROUP, rows), 0)).astype(jnp.float32)

    def take(send, recv, ss, rs, base, out_ref, at):
        @pl.loop(0, GROUP)
        def _(q):
            s = base + q

            @pl.when(s != me)
            def _():
                arrival(send, recv, ss, rs, s).wait_recv()

        got = recv[pl.ds(base, GROUP)].reshape(GROUP * block, piece)
        got = f32dot(perm_ref[...], got).astype(jnp.bfloat16)
        for k in range(PIECES):
            out_ref[at, k * piece:(k + 1) * piece] = got[k * rows:(k + 1) * rows]

    @pl.loop(0, groups)
    def _(i):
        base = ((mine + i) % groups) * GROUP
        at = pl.ds(pl.multiple_of(i * rows, rows), rows)
        take(xsend, xrecv, xs, xr, base, x_ref, at)
        x = x_ref[at, :]
        g = f32dot(x, wg[...], NT)
        u = f32dot(x, wu[...], NT)
        sig = 1.0 / (1.0 + jnp.exp(-g))
        silu = g * sig
        h = (silu * u).astype(jnp.bfloat16)
        h_ref[at, :] = h
        take(dsend, drecv, ds, dr, base, d_ref, at)
        dh = f32dot(d_ref[at, :], wd[...], NT)
        total = jnp.sum(h.astype(jnp.float32) * dh, axis=1, keepdims=True)
        dg = (dh * u * sig * (1.0 + g * (1.0 - sig))).astype(jnp.bfloat16)
        du = (dh * silu).astype(jnp.bfloat16)
        dg_ref[at, :] = dg
        du_ref[at, :] = du
        dx = (f32dot(dg, wg[...]) + f32dot(du, wu[...])).astype(jnp.bfloat16)
        for k in range(PIECES):
            cstack[k * rows:(k + 1) * rows, :] = dx[:, k * piece:(k + 1) * piece]
        bsend[pl.ds(base, GROUP)] = (
            f32dot(unperm_ref[...], cstack[...])
            .astype(jnp.bfloat16)
            .reshape(GROUP, block, piece)
        )
        probs = lax.dot_general(
            gather, jnp.where(keep, total, 0.0), (((1,), (0,)), ((), ())),
            precision=lax.Precision.HIGHEST, preferred_element_type=jnp.float32,
        )
        for q in range(GROUP):
            psend[base + q] = probs[q:q + 1]

        @pl.loop(0, GROUP)
        def _(q):
            d = base + (lane + q) % GROUP

            @pl.when(d != me)
            def _():
                copy(bsend, brecv, bs, br, d).start()
                copy(psend, precv, ps, pr, d).start()

        @pl.when(i == 0)
        def _():
            brecv[me] = bsend[me]
            precv[me] = psend[me]

    for left, right_ref, out_ref in (
        (dg_ref, x_ref, gg_ref), (du_ref, x_ref, gu_ref), (h_ref, d_ref, gd_ref)
    ):
        turned[...] = left[...].T

        @pl.loop(0, PIECES)
        def _(k):
            cols = pl.ds(pl.multiple_of(k * piece, piece), piece)
            out_ref[:, cols] = f32dot(turned[...], right_ref[:, cols]).astype(jnp.bfloat16)

    gsum[...] = jnp.zeros_like(gsum)

    @pl.loop(0, groups)
    def _(i):
        base = ((mine - i + groups) % groups) * GROUP

        @pl.loop(0, GROUP)
        def _(q):
            s = base + q

            @pl.when(s != me)
            def _():
                arrival(bsend, brecv, bs, br, s).wait_recv()
                arrival(psend, precv, ps, pr, s).wait_recv()

            pmat[pl.ds(s, 1), :] = precv[s]

        back = brecv[pl.ds(base, GROUP)].reshape(size, piece)
        at = lax.broadcasted_iota(jnp.int32, (tok, size), 1) + base * block
        for k in range(PIECES):
            route = (at == tgt + k).astype(jnp.float32).astype(jnp.bfloat16)
            gsum[:, k * piece:(k + 1) * piece] += f32dot(route, back)

    gtok_ref[...] = gsum[...].astype(jnp.bfloat16)
    pick = (lax.broadcasted_iota(jnp.int32, (tok, n), 1) == eid.astype(jnp.int32)).astype(jnp.float32)
    found = lax.dot_general(
        pick, pmat[...], (((1,), (0,)), ((), ())),
        precision=lax.Precision.HIGHEST, preferred_element_type=jnp.float32,
    )
    found = jnp.where(
        lax.broadcasted_iota(jnp.int32, (tok, 128), 1) == slot.astype(jnp.int32), found, 0.0
    )
    found = jnp.sum(found, axis=1, keepdims=True)
    gprob_ref[...] = jnp.sum(jnp.where(eye, found, 0.0), axis=0, keepdims=True) / prob_row

    @pl.loop(0, n)
    def _(d):
        @pl.when(d != me)
        def _():
            copy(xsend, xrecv, xs, xr, d).wait_send()
            copy(dsend, drecv, ds, dr, d).wait_send()
            copy(bsend, brecv, bs, br, d).wait_send()
            copy(psend, precv, ps, pr, d).wait_send()


def store_kernel(*refs):
    sem = refs[-1]
    count = len(refs) // 2
    moves = [
        pltpu.make_async_copy(refs[i], refs[count + i], sem.at[i]) for i in range(count)
    ]
    for move in moves:
        move.start()
    for move in moves:
        move.wait()


def on_device(tokens, cotangent, gate_prob, expert_ids, keep_mask, w_gate, w_up, w_down):
    tok, width = tokens.shape
    hidden = w_gate.shape[2]
    n_wide, n_narrow = lax.axis_size("wide"), lax.axis_size("narrow")
    n = n_wide * n_narrow
    cap = max(2, 5 * tok // (4 * n) + 1)
    piece = width // PIECES
    block = cap * PIECES

    owner = jnp.where(keep_mask == 1, expert_ids.reshape(tok), -1).astype(jnp.float32)
    row = jnp.stack([gate_prob, owner])

    vmem = pl.BlockSpec(memory_space=pltpu.VMEM)
    hbm = pl.BlockSpec(memory_space=pl.ANY)
    bf16, f32 = jnp.bfloat16, jnp.float32
    buf = pltpu.VMEM((n, block, piece), bf16)
    small = pltpu.VMEM((n, 1, 128), f32)
    weight = pltpu.VMEM((hidden, width), bf16)
    inner = pltpu.VMEM((n * cap, hidden), bf16)
    parts = pl.pallas_call(
        functools.partial(exchange_kernel, n, n_narrow, cap),
        out_shape=(
            jax.ShapeDtypeStruct((tok, width), bf16),
            jax.ShapeDtypeStruct((1, tok), f32),
            jax.ShapeDtypeStruct((hidden, width), bf16),
            jax.ShapeDtypeStruct((hidden, width), bf16),
            jax.ShapeDtypeStruct((hidden, width), bf16),
        ),
        in_specs=[vmem] * 3 + [hbm] * 3,
        out_specs=(vmem,) * 5,
        scratch_shapes=[
            weight, weight, weight,
            pltpu.VMEM((PIECES * tok, piece), bf16),
            pltpu.VMEM((PIECES * tok, piece), bf16),
            pltpu.VMEM((GROUP * block, piece), bf16),
            pltpu.VMEM((n * cap, width), bf16),
            pltpu.VMEM((n * cap, width), bf16),
            inner, inner, inner,
            pltpu.VMEM((hidden, n * cap), bf16),
            pltpu.VMEM((GROUP * block, GROUP * block), bf16),
            pltpu.VMEM((GROUP * block, GROUP * block), bf16),
            pltpu.VMEM((tok, width), f32),
            buf, buf, buf, buf, buf, buf, small, small,
            pltpu.VMEM((n, 128), f32),
            pltpu.SemaphoreType.DMA((3,)),
        ] + [pltpu.SemaphoreType.DMA((n,))] * 8,
        compiler_params=pltpu.CompilerParams(
            collective_id=0, has_side_effects=True, vmem_limit_bytes=42 * 1024 * 1024
        ),
        name="exchange",
    )(
        tokens, cotangent, row,
        w_gate[0].T, w_up[0].T, w_down[0],
    )
    gtok, gprob, ggate, gup, gdown = pl.pallas_call(
        store_kernel,
        out_shape=[jax.ShapeDtypeStruct(a.shape, a.dtype) for a in parts],
        in_specs=[hbm] * len(parts),
        out_specs=[hbm] * len(parts),
        scratch_shapes=[pltpu.SemaphoreType.DMA((len(parts),))],
        compiler_params=pltpu.CompilerParams(vmem_limit_bytes=1024 * 1024),
        name="store",
    )(*parts)
    return gtok, gprob[0], ggate.T[None], gup.T[None], gdown[None]


def solution(mesh):
    both = ("wide", "narrow")
    return jax.shard_map(
        on_device,
        mesh=mesh,
        in_specs=(
            P(both, None), P(both, None), P(both), P(both, None), P(both),
            P(both, None, None), P(both, None, None), P(both, None, None),
        ),
        out_specs=(
            P(both, None), P(both),
            P(both, None, None), P(both, None, None), P(both, None, None),
        ),
        check_vma=False,
    )
```

```python
import functools

import jax
import jax.numpy as jnp
from jax import lax
from jax.experimental import pallas as pl
from jax.experimental.pallas import tpu as pltpu
from jax.sharding import PartitionSpec as P

GROUP = 8
PIECES = 8
MESH = pl.DeviceIdType.MESH
NT = (((1,), (1,)), ((), ()))
TN = (((0,), (0,)), ((), ()))


def f32dot(a, b, dims=(((1,), (0,)), ((), ()))):
    return lax.dot_general(a, b, dims, preferred_element_type=jnp.float32)


def exchange_kernel(
    n, n_narrow, cap,
    tok_ref, cot_ref, row_ref,
    wg_hbm, wu_hbm, wd_hbm,
    gtok_ref, gprob_ref, gg_ref, gu_ref, gd_ref,
    wg, wu, wd, xstack, dstack, cstack, x_ref, d_ref, h_ref, dg_ref, du_ref, turned,
    perm_ref, unperm_ref, gsum,
    xsend, dsend, bsend, xrecv, drecv, brecv, psend, precv, pmat,
    wsem, xs, xr, ds, dr, bs, br, ps, pr,
):
    wide, narrow = lax.axis_index("wide"), lax.axis_index("narrow")
    me = wide * n_narrow + narrow
    groups = n // GROUP
    mine = me // GROUP
    lane = me % GROUP
    tok = tok_ref.shape[0]
    piece = tok_ref.shape[1] // PIECES
    rows = GROUP * cap
    block = cap * PIECES

    loads = [
        pltpu.make_async_copy(src, dst, wsem.at[i])
        for i, (src, dst) in enumerate(((wg_hbm, wg), (wu_hbm, wu), (wd_hbm, wd)))
    ]
    for load in loads:
        load.start()

    def where(d):
        return (d // n_narrow, d % n_narrow)

    barrier = pltpu.get_barrier_semaphore()

    @pl.loop(1, n)
    def _(i):
        pl.semaphore_signal(
            barrier, inc=1, device_id=where((me + i) % n), device_id_type=MESH
        )

    older = lax.broadcasted_iota(jnp.int32, (tok, tok), 0)
    newer = lax.broadcasted_iota(jnp.int32, (tok, tok), 1)
    eye = older == newer

    def column(row):
        return jnp.sum(jnp.where(eye, row, 0.0), axis=1, keepdims=True)

    prob_row, eid_row = row_ref[0:1, :], row_ref[1:2, :]
    eid = column(eid_row)
    same = eid == eid_row
    slot_row = jnp.sum(
        jnp.where(same & (older < newer), 1.0, 0.0), axis=0, keepdims=True
    )
    slot = jnp.sum(jnp.where(same & (newer < older), 1.0, 0.0), axis=1, keepdims=True)

    def target(e, j):
        return jnp.where(e >= 0.0, e * block + j * PIECES, -1.0 * block).astype(jnp.int32)

    tgt_row, tgt = target(eid_row, slot_row), target(eid, slot)
    prob = column(prob_row)

    for k in range(PIECES):
        cols = slice(k * piece, (k + 1) * piece)
        at = slice(k * tok, (k + 1) * tok)
        xstack[at, :] = tok_ref[:, cols]
        dstack[at, :] = (prob * cot_ref[:, cols].astype(jnp.float32)).astype(
            jnp.bfloat16
        )

    def copy(send, recv, ss, rs, d):
        return pltpu.make_async_remote_copy(
            src_ref=send.at[d], dst_ref=recv.at[me], send_sem=ss.at[d],
            recv_sem=rs.at[me], device_id=where(d), device_id_type=MESH,
        )

    def arrival(send, recv, ss, rs, s):
        return pltpu.make_async_remote_copy(
            src_ref=send.at[s], dst_ref=recv.at[s], send_sem=ss.at[s],
            recv_sem=rs.at[s], device_id=where(s), device_id_type=MESH,
        )

    def fill(i, first):
        g = (mine - i + groups) % groups
        base = g * GROUP
        at = lax.broadcasted_iota(jnp.int32, (GROUP * block, tok), 0) + base * block
        route = jnp.concatenate(
            [
                (at == tgt_row + k).astype(jnp.float32).astype(jnp.bfloat16)
                for k in range(PIECES)
            ],
            axis=1,
        )
        for send, recv, ss, rs, stack in (
            (xsend, xrecv, xs, xr, xstack), (dsend, drecv, ds, dr, dstack)
        ):
            send[pl.ds(base, GROUP)] = (
                f32dot(route, stack[...]).astype(jnp.bfloat16).reshape(GROUP, block, piece)
            )
            if first and send is xsend:
                pl.semaphore_wait(barrier, n - 1)

            @pl.loop(0, GROUP)
            def _(q):
                d = base + (lane + q) % GROUP

                @pl.when(d != me)
                def _():
                    copy(send, recv, ss, rs, d).start()

    fill(0, True)
    xrecv[me] = xsend[me]
    drecv[me] = dsend[me]

    @pl.loop(1, groups)
    def _(i):
        fill(i, False)

    size = GROUP * block
    one = lax.broadcasted_iota(jnp.int32, (size, size), 0)
    other = lax.broadcasted_iota(jnp.int32, (size, size), 1)
    for a, b, out in ((one, other, perm_ref), (other, one, unperm_ref)):
        hit = b == (a % rows) * PIECES + a // rows
        out[...] = hit.astype(jnp.float32).astype(jnp.bfloat16)

    for load in loads:
        load.wait()

    spread = lax.broadcasted_iota(jnp.int32, (rows, 128), 0) % cap
    keep = spread == lax.broadcasted_iota(jnp.int32, (rows, 128), 1)
    owner = lax.broadcasted_iota(jnp.int32, (GROUP, rows), 1) // cap
    gather = (owner == lax.broadcasted_iota(jnp.int32, (GROUP, rows), 0)).astype(jnp.float32)

    def take(send, recv, ss, rs, base, out_ref, at):
        @pl.loop(0, GROUP)
        def _(q):
            s = base + q

            @pl.when(s != me)
            def _():
                arrival(send, recv, ss, rs, s).wait_recv()

        got = recv[pl.ds(base, GROUP)].reshape(GROUP * block, piece)
        got = f32dot(perm_ref[...], got).astype(jnp.bfloat16)
        for k in range(PIECES):
            out_ref[at, k * piece:(k + 1) * piece] = got[k * rows:(k + 1) * rows]

    @pl.loop(0, groups)
    def _(i):
        base = ((mine + i) % groups) * GROUP
        at = pl.ds(pl.multiple_of(i * rows, rows), rows)
        take(xsend, xrecv, xs, xr, base, x_ref, at)
        x = x_ref[at, :]
        g = f32dot(x, wg[...], NT)
        u = f32dot(x, wu[...], NT)
        sig = 1.0 / (1.0 + jnp.exp(-g))
        silu = g * sig
        h = (silu * u).astype(jnp.bfloat16)
        h_ref[at, :] = h
        take(dsend, drecv, ds, dr, base, d_ref, at)
        dh = f32dot(d_ref[at, :], wd[...], NT)
        total = jnp.sum(h.astype(jnp.float32) * dh, axis=1, keepdims=True)
        dg = (dh * u * sig * (1.0 + g * (1.0 - sig))).astype(jnp.bfloat16)
        du = (dh * silu).astype(jnp.bfloat16)
        dg_ref[at, :] = dg
        du_ref[at, :] = du
        dx = (f32dot(dg, wg[...]) + f32dot(du, wu[...])).astype(jnp.bfloat16)
        for k in range(PIECES):
            cstack[k * rows:(k + 1) * rows, :] = dx[:, k * piece:(k + 1) * piece]
        bsend[pl.ds(base, GROUP)] = (
            f32dot(unperm_ref[...], cstack[...])
            .astype(jnp.bfloat16)
            .reshape(GROUP, block, piece)
        )
        probs = lax.dot_general(
            gather, jnp.where(keep, total, 0.0), (((1,), (0,)), ((), ())),
            precision=lax.Precision.HIGHEST, preferred_element_type=jnp.float32,
        )
        for q in range(GROUP):
            psend[base + q] = probs[q:q + 1]

        @pl.loop(0, GROUP)
        def _(q):
            d = base + (lane + q) % GROUP

            @pl.when(d != me)
            def _():
                copy(bsend, brecv, bs, br, d).start()
                copy(psend, precv, ps, pr, d).start()

        @pl.when(i == 0)
        def _():
            brecv[me] = bsend[me]
            precv[me] = psend[me]

    for left, right_ref, out_ref in (
        (dg_ref, x_ref, gg_ref), (du_ref, x_ref, gu_ref), (h_ref, d_ref, gd_ref)
    ):
        turned[...] = left[...].T

        @pl.loop(0, PIECES)
        def _(k):
            cols = pl.ds(pl.multiple_of(k * piece, piece), piece)
            out_ref[:, cols] = f32dot(turned[...], right_ref[:, cols]).astype(jnp.bfloat16)

    gsum[...] = jnp.zeros_like(gsum)

    @pl.loop(0, groups)
    def _(i):
        base = ((mine - i + groups) % groups) * GROUP

        @pl.loop(0, GROUP)
        def _(q):
            s = base + q

            @pl.when(s != me)
            def _():
                arrival(bsend, brecv, bs, br, s).wait_recv()
                arrival(psend, precv, ps, pr, s).wait_recv()

            pmat[pl.ds(s, 1), :] = precv[s]

        back = brecv[pl.ds(base, GROUP)].reshape(size, piece)
        at = lax.broadcasted_iota(jnp.int32, (tok, size), 1) + base * block
        for k in range(PIECES):
            route = (at == tgt + k).astype(jnp.float32).astype(jnp.bfloat16)
            gsum[:, k * piece:(k + 1) * piece] += f32dot(route, back)

    gtok_ref[...] = gsum[...].astype(jnp.bfloat16)
    pick = (lax.broadcasted_iota(jnp.int32, (tok, n), 1) == eid.astype(jnp.int32)).astype(jnp.float32)
    found = lax.dot_general(
        pick, pmat[...], (((1,), (0,)), ((), ())),
        precision=lax.Precision.HIGHEST, preferred_element_type=jnp.float32,
    )
    found = jnp.where(
        lax.broadcasted_iota(jnp.int32, (tok, 128), 1) == slot.astype(jnp.int32), found, 0.0
    )
    found = jnp.sum(found, axis=1, keepdims=True)
    gprob_ref[...] = jnp.sum(jnp.where(eye, found, 0.0), axis=0, keepdims=True) / prob_row

    @pl.loop(0, n)
    def _(d):
        @pl.when(d != me)
        def _():
            copy(xsend, xrecv, xs, xr, d).wait_send()
            copy(dsend, drecv, ds, dr, d).wait_send()
            copy(bsend, brecv, bs, br, d).wait_send()
            copy(psend, precv, ps, pr, d).wait_send()


def store_kernel(*refs):
    sem = refs[-1]
    count = len(refs) // 2
    moves = [
        pltpu.make_async_copy(refs[i], refs[count + i], sem.at[i]) for i in range(count)
    ]
    for move in moves:
        move.start()
    for move in moves:
        move.wait()


def on_device(tokens, cotangent, gate_prob, expert_ids, keep_mask, w_gate, w_up, w_down):
    tok, width = tokens.shape
    hidden = w_gate.shape[2]
    n_wide, n_narrow = lax.axis_size("wide"), lax.axis_size("narrow")
    n = n_wide * n_narrow
    cap = max(2, 5 * tok // (4 * n) + 1)
    piece = width // PIECES
    block = cap * PIECES

    owner = jnp.where(keep_mask == 1, expert_ids.reshape(tok), -1).astype(jnp.float32)
    row = jnp.stack([gate_prob, owner])

    vmem = pl.BlockSpec(memory_space=pltpu.VMEM)
    hbm = pl.BlockSpec(memory_space=pl.ANY)
    bf16, f32 = jnp.bfloat16, jnp.float32
    buf = pltpu.VMEM((n, block, piece), bf16)
    small = pltpu.VMEM((n, 1, 128), f32)
    weight = pltpu.VMEM((hidden, width), bf16)
    inner = pltpu.VMEM((n * cap, hidden), bf16)
    parts = pl.pallas_call(
        functools.partial(exchange_kernel, n, n_narrow, cap),
        out_shape=(
            jax.ShapeDtypeStruct((tok, width), bf16),
            jax.ShapeDtypeStruct((1, tok), f32),
            jax.ShapeDtypeStruct((hidden, width), bf16),
            jax.ShapeDtypeStruct((hidden, width), bf16),
            jax.ShapeDtypeStruct((hidden, width), bf16),
        ),
        in_specs=[vmem] * 3 + [hbm] * 3,
        out_specs=(vmem,) * 5,
        scratch_shapes=[
            weight, weight, weight,
            pltpu.VMEM((PIECES * tok, piece), bf16),
            pltpu.VMEM((PIECES * tok, piece), bf16),
            pltpu.VMEM((GROUP * block, piece), bf16),
            pltpu.VMEM((n * cap, width), bf16),
            pltpu.VMEM((n * cap, width), bf16),
            inner, inner, inner,
            pltpu.VMEM((hidden, n * cap), bf16),
            pltpu.VMEM((GROUP * block, GROUP * block), bf16),
            pltpu.VMEM((GROUP * block, GROUP * block), bf16),
            pltpu.VMEM((tok, width), f32),
            buf, buf, buf, buf, buf, buf, small, small,
            pltpu.VMEM((n, 128), f32),
            pltpu.SemaphoreType.DMA((3,)),
        ] + [pltpu.SemaphoreType.DMA((n,))] * 8,
        compiler_params=pltpu.CompilerParams(
            collective_id=0, has_side_effects=True, vmem_limit_bytes=42 * 1024 * 1024
        ),
        name="exchange",
    )(
        tokens, cotangent, row,
        w_gate[0].T, w_up[0].T, w_down[0],
    )
    gtok, gprob, ggate, gup, gdown = pl.pallas_call(
        store_kernel,
        out_shape=[jax.ShapeDtypeStruct(a.shape, a.dtype) for a in parts],
        in_specs=[hbm] * len(parts),
        out_specs=[hbm] * len(parts),
        scratch_shapes=[pltpu.SemaphoreType.DMA((len(parts),))],
        compiler_params=pltpu.CompilerParams(vmem_limit_bytes=1024 * 1024),
        name="store",
    )(*parts)
    return gtok, gprob[0], ggate.T[None], gup.T[None], gdown[None]


def solution(mesh):
    both = ("wide", "narrow")
    return jax.shard_map(
        on_device,
        mesh=mesh,
        in_specs=(
            P(both, None), P(both, None), P(both), P(both, None), P(both),
            P(both, None, None), P(both, None, None), P(both, None, None),
        ),
        out_specs=(
            P(both, None), P(both),
            P(both, None, None), P(both, None, None), P(both, None, None),
        ),
        check_vma=False,
    )
```
